32 devices in a mesh: fsdp: 8 (over z, core), ctx: 4 (over y, x).
Axes of the slice: x: 2, y: 2, z: 4, core: 2. Of those that a mesh axis runs over, the one named last changes fastest.
Arguments:
- hidden_in: bfloat16 [16384, 1024], P(('fsdp', 'ctx')), may hold values from -6 to 6
- seg_ids: int32 [16384], P(('fsdp', 'ctx')), may hold values from 0 to 4, as said below
- gain_mixer: float32 [1024], replicated, may hold values from 0.5 to 1.5
- gain_ffn: float32 [1024], replicated, may hold values from 0.5 to 1.5
- w_in: bfloat16 [1024, 3352], P('fsdp'), may hold values from -0.1875 to 0.1875
- w_qkv: bfloat16 [1024, 768], P('fsdp'), may hold values from -0.1875 to 0.1875
- w_attn_out: bfloat16 [512, 1024], P('fsdp'), may hold values from -4 to 4
- w_ssm_out: bfloat16 [1536, 1024], P('fsdp'), may hold values from -0.01953125 to 0.01953125
- w_gate_up: bfloat16 [1024, 4096], P('fsdp'), may hold values from -0.1875 to 0.1875
- w_down: bfloat16 [2048, 1024], P('fsdp'), may hold values from -0.125 to 0.125
- dt_bias: float32 [24], replicated, may hold values from -5 to -2.5
- a_log: float32 [24], replicated, may hold values from -7 to 0
- d_skip: float32 [24], replicated, may hold values from 0.5 to 1.5
- out_grad: bfloat16 [16384, 1024], P(('fsdp', 'ctx')), may hold values from -6 to 6
Outputs:
- output: bfloat16 [16384, 1024], P(('fsdp', 'ctx'))
- grad_in: float32 [16384, 1024], P(('fsdp', 'ctx'))
- grad_gain_mixer: float32 [1024], P('fsdp')
- grad_gain_ffn: float32 [1024], P('fsdp')
- grad_w_in: float32 [1024, 3352], P('fsdp')
- grad_w_qkv: float32 [1024, 768], P('fsdp')
- grad_w_attn_out: float32 [512, 1024], P('fsdp')
- grad_w_ssm_out: float32 [1536, 1024], P('fsdp')
- grad_w_gate_up: float32 [1024, 4096], P('fsdp')
- grad_w_down: float32 [2048, 1024], P('fsdp')
- grad_dt_bias: float32 [24], replicated
- grad_a_log: float32 [24], replicated
- grad_d_skip: float32 [24], replicated
The draws below stay inside these ranges and needn't reach their ends.
Inputs may be any that keep to these rules, and one draw needn't show every extreme that they name: `seg_ids`: within each group of 2048 tokens the ids start at 0, never fall and rise by one at a sequence's start; every group holds ids 0 to 4; sequences 0 and 1 lie within the group's first 512 tokens, sequences 3 and 4 within its last 512, so sequence 2 runs from the first of the group's devices to its last.
All inputs are finite; a program needn't handle non-finite values.
Results may differ from the reference program's by a relative error of at most 0.02.
Values may be sent and summed in bfloat16 or wider, within the bound.
No kernel may reach another device: no remote copies, remote signals or barrier semaphores. Data moves between devices by JAX's collectives and lax.ppermute only.
A program may use at most 384 MiB of HBM per device.

```python
import jax
import jax.numpy as jnp
from jax import lax

D = 1024
FF = 2048
QUERY_HEADS = 8
KEY_VALUE_HEADS = 2
HEAD_WIDTH = 64
MH = 24
PD = 64
ST = 128
TOK_DEV = 512
D_SSM = 1536
IN_COLS = 3352
QKV_COLS = 768
GROUP = 2048
TOKENS = 16384


def draw_seg_ids(key, part):
    key = jax.random.fold_in(key, 11)
    query_groups = TOKENS // GROUP
    half = TOK_DEV // 2
    key_one, key_two, key_three, key_four = jax.random.split(key, 4)
    cut_one = jax.random.randint(key_one, (query_groups, 1), 1, half + 1)
    cut_two = cut_one + jax.random.randint(key_two, (query_groups, 1), 1, half)
    cut_three = GROUP - TOK_DEV + jax.random.randint(key_three, (query_groups, 1), 1, half + 1)
    cut_four = cut_three + jax.random.randint(key_four, (query_groups, 1), 1, half)
    place = jnp.arange(GROUP, dtype=jnp.int32)[None, :]
    ids = (place >= cut_one).astype(jnp.int32) + (place >= cut_two).astype(jnp.int32)
    ids = ids + (place >= cut_three).astype(jnp.int32) + (place >= cut_four).astype(jnp.int32)
    return ids.reshape(TOKENS).astype(jnp.int32)


def steps_of(rng, shape, shards, low, top_value):
    level, own = 1.0, jax.random.fold_in(rng, 6)
    for dim, blocks in shards:
        heights = jnp.exp(jax.random.uniform(jax.random.fold_in(own, dim), (blocks,), jnp.float32, low / len(shards), top_value / len(shards)))
        level = level * jnp.repeat(heights, shape[dim] // blocks).reshape([-1 if axis == dim else 1 for axis in range(len(shape))])
    return level


def gaussian(own_key, extent, scale, limit, cuts=(), held_as=jnp.bfloat16):
    entries = jax.random.normal(own_key, extent, jnp.float32) * scale
    if len(cuts) > 0:
        entries = steps_of(own_key, extent, cuts, -0.22, 0.18) * entries
    return jnp.clip(entries, min=-limit, max=limit).astype(held_as)


def setup_inputs(seed: int = 0) -> dict:
    key_of = jax.random.split(jax.random.key(seed), 15)
    return {
        "hidden_in": gaussian(key_of[0], (TOKENS, D), 1.0, 6.0, ((0, 32),)),
        "seg_ids": draw_seg_ids(jax.random.fold_in(key_of[14], 71), 0),
        "gain_mixer": jnp.clip(1.0 + 0.1 * jax.random.normal(key_of[2], (D,), jnp.float32), 0.5, 1.5),
        "gain_ffn": jnp.clip(1.0 + 0.1 * jax.random.normal(key_of[3], (D,), jnp.float32), 0.5, 1.5),
        "w_in": gaussian(key_of[4], (D, IN_COLS), D ** -0.5, 0.1875, ((0, 8),)),
        "w_qkv": gaussian(key_of[5], (D, QKV_COLS), D ** -0.5, 0.1875, ((0, 8),)),
        "w_attn_out": gaussian(key_of[6], (QUERY_HEADS * HEAD_WIDTH, D), 2 ** -0.5, 4.0, ((0, 8),)),
        "w_ssm_out": gaussian(key_of[7], (D_SSM, D), (D_SSM * 64) ** -0.5, 0.01953125, ((0, 8),)),
        "w_gate_up": gaussian(key_of[8], (D, 2 * FF), D ** -0.5, 0.1875, ((0, 8),)),
        "w_down": gaussian(key_of[9], (FF, D), FF ** -0.5, 0.125, ((0, 8),)),
        "dt_bias": jnp.clip(jax.random.uniform(key_of[10], (MH,), jnp.float32, -5.0, -2.5), -5.0, -2.5),
        "a_log": jnp.clip(jax.random.uniform(key_of[11], (MH,), jnp.float32, -7.0, 0.0), -7.0, 0.0),
        "d_skip": jnp.clip(jax.random.uniform(key_of[12], (MH,), jnp.float32, 0.5, 1.5), 0.5, 1.5),
        "out_grad": gaussian(key_of[13], (TOKENS, D), 1.0, 6.0, ((0, 32),)),
    }


EPS = 1e-05
ROPE_BASE = 100000000000.0
HIGH = lax.Precision.HIGHEST

@jax.custom_vjp
def reduced_precision(v):
    return lax.optimization_barrier(v.astype(jnp.bfloat16)).astype(jnp.float32)

@jax.custom_vjp
def low_back(v):
    return v

def low_keep(v):
    return (reduced_precision(v), None)

def low_pass(kept, grad):
    return (grad,)

def back_keep(v):
    return (v, None)

def back_low(kept, grad):
    return (reduced_precision(grad),)
reduced_precision.defvjp(low_keep, low_pass)
low_back.defvjp(back_keep, back_low)

def matmul(left, right):
    return jnp.dot(left, right, precision=HIGH)

def rms_scale(value_rows, gain):
    return value_rows * lax.rsqrt(lax.optimization_barrier(jnp.mean(value_rows * value_rows, axis=-1, keepdims=True)) + EPS) * gain

def rope_tables(positions):
    half = HEAD_WIDTH // 2
    freqs = ROPE_BASE ** (-(jnp.arange(half, dtype=jnp.float32) * 2.0) / HEAD_WIDTH)
    angles = positions.astype(jnp.float32)[:, None] * freqs[None, :]
    return (jnp.cos(angles), jnp.sin(angles))

def apply_rotary(value_rows, cosine_table, sine_table):
    half = value_rows.shape[-1] // 2
    leading = value_rows[..., :half]
    trailing = value_rows[..., half:]
    cos_part = cosine_table[:, None, :]
    sin_part = sine_table[:, None, :]
    return jnp.concatenate([leading * cos_part - trailing * sin_part, trailing * cos_part + leading * sin_part], axis=-1)

def ssd_blocks(x_heads, b_vals, c_vals, steps, logd, segment_labels, span):
    count = x_heads.shape[0]
    heads = x_heads.shape[1]
    dims = x_heads.shape[2]
    states = b_vals.shape[1]
    block_count = count // span
    order = jnp.arange(span)
    lower = order[:, None] >= order[None, :]

    def step(carry, item):
        state, last = carry
        x_block, b_block, c_block, dt_block, log_block, seg_block = item
        cumul = jnp.cumsum(log_block, axis=0)
        same = lower & (seg_block[:, None] == seg_block[None, :])
        gap = jnp.where(same[:, :, None], cumul[:, None, :] - cumul[None, :, :], 0.0)
        decay = jnp.where(same[:, :, None], jnp.exp(gap), 0.0)
        inner = jnp.dot(c_block, b_block.T, precision=HIGH)
        mixing = decay * inner[:, :, None]
        scaled = x_block * dt_block[:, :, None]
        result = jnp.einsum('tsh,shp->thp', mixing, scaled, precision=HIGH)
        keep = jnp.exp(cumul) * (seg_block == last).astype(jnp.float32)[:, None]
        result = result + keep[:, :, None] * jnp.einsum('tn,hpn->thp', c_block, state, precision=HIGH)
        tail = (seg_block == seg_block[-1]).astype(jnp.float32)[:, None] * jnp.exp(cumul[-1][None, :] - cumul)
        fresh = jnp.einsum('sh,shp,sn->hpn', tail * dt_block, x_block, b_block, precision=HIGH)
        state = keep[-1][:, None, None] * state + fresh
        return ((state, seg_block[-1]), result)
    init = (jnp.zeros((heads, dims, states), jnp.float32), jnp.full((), -1, jnp.int32))
    items = (x_heads.reshape(block_count, span, heads, dims), b_vals.reshape(block_count, span, states), c_vals.reshape(block_count, span, states), steps.reshape(block_count, span, heads), logd.reshape(block_count, span, heads), segment_labels.reshape(block_count, span))
    (state, last), results = lax.scan(jax.checkpoint(step), init, items)
    return (results.reshape(count, heads, dims), state)

def attention_layer(query_rows, key_rows, value_rows, segment_labels, index_rows):
    total_length = query_rows.shape[0]
    rows_block = min(512, total_length)
    block_count = total_length // rows_block
    scale = HEAD_WIDTH ** (-0.5)

    def one_block(item):
        query_block, seg_block, index_block = item
        scores = low_back(jnp.einsum('qgrd,kgd->qgrk', query_block, key_rows, precision=HIGH) * scale)
        allowed = (seg_block[:, None] == segment_labels[None, :]) & (index_rows[None, :] <= index_block[:, None])
        masked = jnp.where(allowed[:, None, None, :], scores, -1e+30)
        top = lax.optimization_barrier(jnp.max(masked, axis=-1, keepdims=True))
        lse = top + jnp.log(lax.optimization_barrier(jnp.sum(jnp.exp(masked - top), axis=-1, keepdims=True)))
        probs = reduced_precision(jnp.exp(masked - lse))
        return jnp.einsum('qgrk,kgd->qgrd', probs, value_rows, precision=HIGH)
    shaped = query_rows.reshape((block_count, rows_block) + query_rows.shape[1:])
    result = lax.map(jax.checkpoint(one_block), (shaped, segment_labels.reshape(block_count, rows_block), index_rows.reshape(block_count, rows_block)))
    return result.reshape(query_rows.shape)

def layer(inputs, segment_labels, params):
    gain_mixer, gain_ffn, w_in, w_qkv, w_attn_out, w_ssm_out, w_gate_up, w_down, dt_bias, a_log, d_skip = params
    total_length = inputs.shape[0]
    ssm_width = MH * PD
    index_rows = jnp.arange(total_length, dtype=jnp.int32)
    earlier = jnp.concatenate([jnp.full((1,), -1, jnp.int32), segment_labels[:-1]])
    starts = lax.cummax(jnp.where(segment_labels != earlier, index_rows, 0), axis=0)
    cosine_table, sine_table = rope_tables(index_rows - starts)
    normed = reduced_precision(rms_scale(inputs, gain_mixer))
    projected = low_back(matmul(normed, w_in))
    gate_z = projected[:, :ssm_width]
    x_heads = reduced_precision(projected[:, ssm_width:2 * ssm_width]).reshape(total_length, MH, PD)
    b_vals = reduced_precision(projected[:, 2 * ssm_width:2 * ssm_width + ST])
    c_vals = reduced_precision(projected[:, 2 * ssm_width + ST:2 * ssm_width + 2 * ST])
    dt_raw = projected[:, 2 * ssm_width + 2 * ST:]
    query_key_value = low_back(matmul(normed, w_qkv))
    query_rows = reduced_precision(apply_rotary(query_key_value[:, :QUERY_HEADS * HEAD_WIDTH].reshape(total_length, QUERY_HEADS, HEAD_WIDTH), cosine_table, sine_table))
    key_rows = reduced_precision(apply_rotary(query_key_value[:, QUERY_HEADS * HEAD_WIDTH:(QUERY_HEADS + KEY_VALUE_HEADS) * HEAD_WIDTH].reshape(total_length, KEY_VALUE_HEADS, HEAD_WIDTH), cosine_table, sine_table))
    value_rows = reduced_precision(query_key_value[:, (QUERY_HEADS + KEY_VALUE_HEADS) * HEAD_WIDTH:].reshape(total_length, KEY_VALUE_HEADS, HEAD_WIDTH))
    attended_rows = attention_layer(query_rows.reshape(total_length, KEY_VALUE_HEADS, QUERY_HEADS // KEY_VALUE_HEADS, HEAD_WIDTH), key_rows, value_rows, segment_labels, index_rows)
    attended_rows = reduced_precision(low_back(attended_rows.reshape(total_length, QUERY_HEADS * HEAD_WIDTH)))
    attn_branch = low_back(matmul(attended_rows, w_attn_out))
    steps = jax.nn.softplus(dt_raw + dt_bias)
    logd = -steps * jnp.exp(a_log)
    scanned, unused = ssd_blocks(x_heads, b_vals, c_vals, steps, logd, segment_labels, min(256, TOK_DEV))
    mixed = scanned + d_skip[None, :, None] * x_heads
    gated = reduced_precision(low_back((mixed * jax.nn.silu(gate_z.reshape(total_length, MH, PD))).reshape(total_length, ssm_width)))
    ssm_branch = low_back(matmul(gated, w_ssm_out))
    middle = inputs + attn_branch + ssm_branch
    normed_ffn = reduced_precision(rms_scale(middle, gain_ffn))
    gate_up = low_back(matmul(normed_ffn, w_gate_up))
    hidden = reduced_precision(jax.nn.silu(gate_up[:, :FF]) * gate_up[:, FF:])
    return middle + low_back(matmul(hidden, w_down))

def reference(hidden_in, seg_ids, gain_mixer, gain_ffn, w_in, w_qkv, w_attn_out, w_ssm_out, w_gate_up, w_down, dt_bias, a_log, d_skip, out_grad):
    query_groups = TOKENS // GROUP
    params = (gain_mixer, gain_ffn, w_in.astype(jnp.float32), w_qkv.astype(jnp.float32), w_attn_out.astype(jnp.float32), w_ssm_out.astype(jnp.float32), w_gate_up.astype(jnp.float32), w_down.astype(jnp.float32), dt_bias, a_log, d_skip)
    inputs = hidden_in.astype(jnp.float32).reshape(query_groups, GROUP, D)
    seg_groups = seg_ids.reshape(query_groups, GROUP)

    def forward(inputs, params):

        def one_group(item):
            return layer(item[0], item[1], params)
        return lax.map(one_group, (inputs, seg_groups))
    result, pullback = jax.vjp(forward, inputs, params)
    input_grad, grads = pullback(out_grad.astype(jnp.float32).reshape(query_groups, GROUP, D))
    return (result.reshape(TOKENS, D).astype(jnp.bfloat16), input_grad.reshape(TOKENS, D), grads[0], grads[1], grads[2], grads[3], grads[4], grads[5], grads[6], grads[7], grads[8], grads[9], grads[10])
```

```python
import functools

import jax
import jax.numpy as jnp
from jax import lax
from jax.experimental import pallas as pl
from jax.experimental.pallas import tpu as pltpu
from jax.sharding import PartitionSpec as P

FF = 2048
QUERY_HEADS = 8
KEY_VALUE_HEADS = 2
HEAD_WIDTH = 64
MH = 24
PD = 64
ST = 128
D_SSM = MH * PD
PAIRS = MH // 2
LANES = 128

EPS = 1e-05
ROPE_BASE = 100000000000.0
HIGH = lax.Precision.HIGHEST
F32 = jnp.float32
BF16 = jnp.bfloat16

NN = ((1,), (0,))
NT = ((1,), (1,))
TN = ((0,), (0,))
FLOW_ROWS = 16
VMEM_LIMIT = 56 * 1024 * 1024


def mm(left, right, dims=NN, precision=None):
    return lax.dot_general(
        left, right, (dims, ((), ())), precision=precision, preferred_element_type=F32
    )


def params(*semantics):
    return pltpu.CompilerParams(
        dimension_semantics=semantics or None, vmem_limit_bytes=VMEM_LIMIT
    )


def behind(kernel, inputs, extra):
    if not extra:
        return kernel

    def run(*refs):
        kernel(*refs[:inputs], *refs[inputs + extra :])

    return run


def anywhere(count):
    return [pl.BlockSpec(memory_space=pl.ANY)] * count


def smem():
    return pl.BlockSpec(memory_space=pltpu.SMEM)


def whole():
    return pl.BlockSpec(memory_space=pltpu.VMEM)


def swap_halves(block):
    half = HEAD_WIDTH // 2
    lane = lax.broadcasted_iota(jnp.int32, block.shape, 1)
    ahead = pltpu.roll(block, LANES - half, 1)
    behind = pltpu.roll(block, half, 1)
    return jnp.where(lax.rem(lane, HEAD_WIDTH) < half, ahead, behind)


def rotate_kernel(qkv_ref, cos_ref, sin_ref, q_ref, kv_ref):
    cos, sin = cos_ref[...], sin_ref[...]
    q_cols = QUERY_HEADS * HEAD_WIDTH
    for start in range(0, q_cols, LANES):
        block = qkv_ref[:, start : start + LANES]
        turned = (block * cos + swap_halves(block) * sin).astype(BF16)
        q_ref[:, start : start + LANES] = turned * jnp.asarray(HEAD_WIDTH**-0.5, BF16)
    block = qkv_ref[:, q_cols : q_cols + LANES]
    keys = block * cos + swap_halves(block) * sin
    values = qkv_ref[:, q_cols + LANES :]
    lane = lax.broadcasted_iota(jnp.int32, keys.shape, 1)
    first = lane < HEAD_WIDTH
    kv_ref[0] = jnp.where(first, keys, pltpu.roll(values, HEAD_WIDTH, 1)).astype(BF16)
    kv_ref[1] = jnp.where(first, pltpu.roll(keys, HEAD_WIDTH, 1), values).astype(BF16)


def rotate(qkv, cos, sin):
    rows = qkv.shape[0]
    return pl.pallas_call(
        rotate_kernel,
        out_shape=(
            jax.ShapeDtypeStruct((rows, QUERY_HEADS * HEAD_WIDTH), BF16),
            jax.ShapeDtypeStruct((KEY_VALUE_HEADS, rows, LANES), BF16),
        ),
        in_specs=[whole()] * 3,
        out_specs=(whole(), whole()),
        compiler_params=params(),
        name="rotate",
    )(qkv, cos, sin)


def unrotate_kernel(dq_ref, dkv_ref, cos_ref, sin_ref, out_ref):
    cos, sin = cos_ref[...], sin_ref[...]
    q_cols = QUERY_HEADS * HEAD_WIDTH
    for start in range(0, q_cols, LANES):
        block = dq_ref[:, start : start + LANES]
        out_ref[:, start : start + LANES] = (block * cos - swap_halves(block) * sin).astype(BF16)
    zero = dkv_ref[0].astype(F32)
    one = dkv_ref[1].astype(F32)
    lane = lax.broadcasted_iota(jnp.int32, zero.shape, 1)
    first = lane < HEAD_WIDTH
    keys = jnp.where(first, zero, pltpu.roll(one, HEAD_WIDTH, 1))
    values = jnp.where(first, pltpu.roll(zero, HEAD_WIDTH, 1), one)
    out_ref[:, q_cols : q_cols + LANES] = (keys * cos - swap_halves(keys) * sin).astype(BF16)
    out_ref[:, q_cols + LANES :] = values.astype(BF16)


def unrotate(dq, dkv, cos, sin):
    rows = dq.shape[0]
    return pl.pallas_call(
        unrotate_kernel,
        out_shape=jax.ShapeDtypeStruct((rows, dq.shape[1] + 2 * LANES), BF16),
        in_specs=[whole()] * 4,
        out_specs=whole(),
        compiler_params=params(),
        name="unrotate",
    )(dq, dkv, cos, sin)


def visible(key_block, place, rows, start):
    key_index = key_block * rows + lax.broadcasted_iota(jnp.int32, (rows, rows), 0)
    query_index = place * rows + lax.broadcasted_iota(jnp.int32, (1, rows), 1)
    return (key_index >= start) & (key_index <= query_index)


def attend_kernel(place_ref, q_ref, kv_ref, start_ref, o_ref, lse_ref, top_s, mass_s, acc_s):
    rows = q_ref.shape[0]
    place = place_ref[0]
    share = QUERY_HEADS // KEY_VALUE_HEADS
    top_s[...] = jnp.full(top_s.shape, -1e30, F32)
    mass_s[...] = jnp.zeros(mass_s.shape, F32)
    acc_s[...] = jnp.zeros(acc_s.shape, F32)
    start = start_ref[...]

    def block(back, unused):
        keys = kv_ref[back, 0, :, :HEAD_WIDTH]
        values = kv_ref[back, 0, :, HEAD_WIDTH:]
        seen = visible(place - back, place, rows, start)
        for r in range(share):
            queries = q_ref[:, r * HEAD_WIDTH : (r + 1) * HEAD_WIDTH]
            scores = jnp.where(seen, mm(keys, queries, NT), -1e30)
            old = top_s[r : r + 1, :]
            new = jnp.maximum(old, jnp.max(scores, axis=0, keepdims=True))
            probs = jnp.exp(scores - new)
            scale = jnp.exp(old - new)
            top_s[r : r + 1, :] = new
            mass_s[r : r + 1, :] = mass_s[r : r + 1, :] * scale + jnp.sum(
                probs, axis=0, keepdims=True
            )
            at = slice(r * HEAD_WIDTH, (r + 1) * HEAD_WIDTH)
            acc_s[at, :] = acc_s[at, :] * scale + mm(values, probs.astype(BF16), TN)
        return unused

    lax.fori_loop(0, place + 1, block, 0)
    lse_ref[0] = top_s[...] + jnp.log(mass_s[...])
    for r in range(share):
        at = slice(r * HEAD_WIDTH, (r + 1) * HEAD_WIDTH)
        acc_s[at, :] = acc_s[at, :] / mass_s[r : r + 1, :]
    o_ref[...] = jnp.transpose(acc_s[...])


def attend(place, q, kv_all, start):
    rows = q.shape[0]
    blocks = kv_all.shape[0]
    share = QUERY_HEADS // KEY_VALUE_HEADS
    wide = share * HEAD_WIDTH
    return pl.pallas_call(
        attend_kernel,
        grid=(KEY_VALUE_HEADS,),
        out_shape=(
            jax.ShapeDtypeStruct(q.shape, F32),
            jax.ShapeDtypeStruct((KEY_VALUE_HEADS, share, rows), F32),
        ),
        in_specs=[
            smem(),
            pl.BlockSpec((rows, wide), lambda g: (0, g)),
            pl.BlockSpec((blocks, 1, rows, LANES), lambda g: (0, g, 0, 0)),
            pl.BlockSpec((1, rows), lambda g: (0, 0)),
        ],
        out_specs=(
            pl.BlockSpec((rows, wide), lambda g: (0, g)),
            pl.BlockSpec((1, share, rows), lambda g: (g, 0, 0)),
        ),
        scratch_shapes=[
            pltpu.VMEM((share, rows), F32),
            pltpu.VMEM((share, rows), F32),
            pltpu.VMEM((wide, rows), F32),
        ],
        compiler_params=params("arbitrary"),
        name="attend",
    )(place, q, kv_all, start)


def attend_back_kernel(
    place_ref, q_ref, kv_ref, start_ref, lse_ref, o_ref, do_ref, dq_ref, dkv_ref, delta_s, dq_s
):
    rows = q_ref.shape[0]
    place = place_ref[0]
    share = QUERY_HEADS // KEY_VALUE_HEADS
    back = pl.program_id(1)

    @pl.when(back == 0)
    def begin():
        flat = jnp.transpose(do_ref[...].astype(F32) * o_ref[...])
        for r in range(share):
            at = slice(r * HEAD_WIDTH, (r + 1) * HEAD_WIDTH)
            delta_s[r : r + 1, :] = jnp.sum(flat[at, :], axis=0, keepdims=True)
        dq_s[...] = jnp.zeros(dq_s.shape, F32)

    @pl.when(back <= place)
    def work():
        keys = kv_ref[0, 0, :, :HEAD_WIDTH]
        values = kv_ref[0, 0, :, HEAD_WIDTH:]
        seen = visible(place - back, place, rows, start_ref[...])
        d_keys = jnp.zeros((rows, HEAD_WIDTH), F32)
        d_values = jnp.zeros((rows, HEAD_WIDTH), F32)
        for r in range(share):
            at = slice(r * HEAD_WIDTH, (r + 1) * HEAD_WIDTH)
            queries = q_ref[:, at]
            d_out = do_ref[:, at]
            scores = mm(keys, queries, NT)
            probs = jnp.where(seen, jnp.exp(scores - lse_ref[0, r : r + 1, :]), 0.0)
            d_values = d_values + mm(probs.astype(BF16), d_out)
            d_probs = mm(values, d_out, NT)
            d_scores = (probs * (d_probs - delta_s[r : r + 1, :])).astype(BF16)
            d_keys = d_keys + mm(d_scores, queries)
            dq_s[at, :] = dq_s[at, :] + mm(keys, d_scores, TN)
        dkv_ref[0, 0] = jnp.concatenate([d_keys, d_values], axis=1).astype(BF16)

    @pl.when(back > place)
    def nothing():
        dkv_ref[0, 0] = jnp.zeros((rows, LANES), BF16)

    @pl.when(back == pl.num_programs(1) - 1)
    def end():
        dq_ref[...] = jnp.transpose(dq_s[...]) * HEAD_WIDTH**-0.5


def attend_back(place, q, kv_all, start, lse, o, d_o, after=()):
    rows = q.shape[0]
    blocks = kv_all.shape[0]
    share = QUERY_HEADS // KEY_VALUE_HEADS
    wide = share * HEAD_WIDTH
    side = pl.BlockSpec((rows, wide), lambda g, j: (0, g))
    block = pl.BlockSpec((1, 1, rows, LANES), lambda g, j: (j, g, 0, 0))
    return pl.pallas_call(
        behind(attend_back_kernel, 7, len(after)),
        grid=(KEY_VALUE_HEADS, blocks),
        out_shape=(
            jax.ShapeDtypeStruct(q.shape, F32),
            jax.ShapeDtypeStruct(kv_all.shape, BF16),
        ),
        in_specs=[
            smem(),
            side,
            block,
            pl.BlockSpec((1, rows), lambda g, j: (0, 0)),
            pl.BlockSpec((1, share, rows), lambda g, j: (g, 0, 0)),
            side,
            side,
        ]
        + anywhere(len(after)),
        out_specs=(side, block),
        scratch_shapes=[pltpu.VMEM((share, rows), F32), pltpu.VMEM((wide, rows), F32)],
        compiler_params=params("arbitrary", "arbitrary"),
        name="attend_back",
    )(place, q, kv_all, start, lse, o, d_o, *after)


LANE_DT, LANE_CUM, LANE_KEEP, LANE_TAIL = 0, 32, 64, 96


def chunk_of(rows):
    return min(256, rows)


def triangle(size, lower):
    row = lax.broadcasted_iota(jnp.int32, (size, size), 0)
    col = lax.broadcasted_iota(jnp.int32, (size, size), 1)
    return (row >= col if lower else row <= col).astype(F32)


def pair_wide(pack, lane):
    rows = pack.shape[0]
    at = lax.broadcasted_iota(jnp.int32, (rows, LANES), 1)
    return jnp.where(at < PD, pack[:, lane : lane + 1], pack[:, lane + 1 : lane + 2])


def softplus(value):
    return jnp.maximum(value, 0.0) + jnp.log1p(jnp.exp(-jnp.abs(value)))


def flow_rows(flow):
    row = lax.broadcasted_iota(jnp.int32, (FLOW_ROWS, flow.shape[1]), 0)
    high = flow.astype(BF16).astype(F32)
    middle = (flow - high).astype(BF16).astype(F32)
    low = flow - high - middle
    parts = jnp.where(row == 0, high, jnp.where(row == 1, middle, jnp.where(row == 2, low, 0.0)))
    return parts.astype(BF16)


def ssm_state_kernel(
    prev_ref, dtr_ref, bias_ref, alog_ref, seg_ref, x_ref, b_ref, pack_ref, flip_ref, far_ref,
    state_ref,
):
    rows = dtr_ref.shape[0]
    span = chunk_of(rows)
    count = rows // span
    dt = softplus(dtr_ref[...] + bias_ref[...])
    logd = -dt * jnp.exp(alog_ref[...])
    lower = triangle(span, True)
    gap = jnp.zeros((span, 32 - MH), F32)
    keeps, tails = [], []
    for c in range(count):
        at = slice(c * span, (c + 1) * span)
        cum = mm(lower, logd[at], precision=HIGH)
        seg = seg_ref[at, :]
        before = prev_ref[0] if c == 0 else seg_ref[c * span - 1 : c * span, :]
        keep = jnp.where(seg == before, jnp.exp(cum), 0.0)
        tail = jnp.where(seg == seg[span - 1 : span, :], jnp.exp(cum[span - 1 : span] - cum), 0.0)
        pack = jnp.concatenate([dt[at], gap, cum, gap, keep, gap, tail, gap], axis=1)
        pack_ref[at, :] = pack
        flip_ref[:, at] = jnp.transpose(pack)
        keeps.append(keep)
        tails.append(tail)
    flow = jnp.ones((1, MH), F32)
    far = []
    for c in range(count):
        far.append(keeps[c] * flow)
        flow = flow * keeps[c][span - 1 : span]
    far_ref[...] = jnp.concatenate(
        [jnp.concatenate(far, axis=0), jnp.zeros((rows, LANES - MH), F32)], axis=1
    )
    after = jnp.ones((1, MH), F32)
    weights = [None] * count
    for c in reversed(range(count)):
        weights[c] = tails[c] * dt[c * span : (c + 1) * span] * after
        after = after * keeps[c][span - 1 : span]
    weight = jnp.concatenate(weights, axis=0)
    b_vals = b_ref[...]
    for j in range(PAIRS):
        at = slice(j * LANES, (j + 1) * LANES)
        scaled = (x_ref[:, at].astype(F32) * pair_wide(weight, 2 * j)).astype(BF16)
        state_ref[:ST, at] = mm(b_vals, scaled, TN).astype(BF16)
        state_ref[ST:, at] = flow_rows(pair_wide(flow, 2 * j))


def ssm_state(prev, dt_raw, bias, a_log, seg_col, x, b_vals):
    rows = dt_raw.shape[0]
    return pl.pallas_call(
        ssm_state_kernel,
        out_shape=(
            jax.ShapeDtypeStruct((rows, LANES), F32),
            jax.ShapeDtypeStruct((LANES, rows), F32),
            jax.ShapeDtypeStruct((rows, LANES), F32),
            jax.ShapeDtypeStruct((ST + FLOW_ROWS, D_SSM), BF16),
        ),
        in_specs=[smem()] + [whole()] * 6,
        out_specs=(whole(),) * 4,
        compiler_params=params(),
        name="ssm_state",
    )(prev, dt_raw, bias, a_log, seg_col, x, b_vals)


def same_lower(seg_col, seg_row, span, transposed):
    row = lax.broadcasted_iota(jnp.int32, (span, span), 0)
    col = lax.broadcasted_iota(jnp.int32, (span, span), 1)
    order = row <= col if transposed else row >= col
    return order & (seg_col == seg_row)


def ssm_forward_kernel(
    pack_ref, flip_ref, segc_ref, segr_ref, x_ref, b_ref, c_ref, z_ref, skip_ref, enter_ref,
    gated_ref, y_ref, inner_s,
):
    rows = x_ref.shape[0]
    span = chunk_of(rows)
    count = rows // span
    j = pl.program_id(0)

    @pl.when(j == 0)
    def begin():
        for c in range(count):
            at = slice(c * span, (c + 1) * span)
            mask = same_lower(segc_ref[at, :], segr_ref[:, at], span, False)
            inner_s[c] = jnp.where(mask, mm(c_ref[at, :], b_ref[at, :], NT), 0.0)

    lane = lax.broadcasted_iota(jnp.int32, (span, LANES), 1)
    state = enter_ref[...]
    for c in range(count):
        at = slice(c * span, (c + 1) * span)
        pack = pltpu.roll(pack_ref[at, :], lax.rem(LANES - 2 * j, LANES), 1)
        x = x_ref[at, :].astype(F32)
        scaled = x * pair_wide(pack, LANE_DT)
        scaled_low = scaled.astype(BF16)
        keep = pair_wide(pack, LANE_KEEP)
        mixed = keep * mm(c_ref[at, :], state.astype(BF16))
        parts = []
        for k in range(2):
            column = pack[:, LANE_CUM + k : LANE_CUM + k + 1]
            row = flip_ref[pl.ds(LANE_CUM + 2 * j + k, 1), at]
            mixing = inner_s[c] * jnp.exp(jnp.minimum(column - row, 0.0))
            parts.append(mm(mixing.astype(BF16), scaled_low))
        mixed = mixed + jnp.where(lane < PD, parts[0], parts[1])
        mixed = mixed + skip_ref[:, :] * x
        y_ref[at, :] = mixed
        z = z_ref[at, :]
        gated_ref[at, :] = (mixed * (z * jax.nn.sigmoid(z))).astype(BF16)
        if c + 1 < count:
            tail = pair_wide(pack, LANE_TAIL)
            fresh = mm(b_ref[at, :], (tail * scaled).astype(BF16), TN)
            state = keep[span - 1 : span, :] * state + fresh


def pair_block(rows):
    return pl.BlockSpec((rows, LANES), lambda j: (0, j))


def held(shape):
    return pl.BlockSpec(shape, lambda j: (0,) * len(shape))


def ssm_forward(pack, flip, seg_col, seg_row, x, b_vals, c_vals, z, skip_wide, enter):
    rows = x.shape[0]
    span = chunk_of(rows)
    return pl.pallas_call(
        ssm_forward_kernel,
        grid=(PAIRS,),
        out_shape=(
            jax.ShapeDtypeStruct((rows, D_SSM), BF16),
            jax.ShapeDtypeStruct((rows, D_SSM), F32),
        ),
        in_specs=[
            held(pack.shape),
            held(flip.shape),
            held(seg_col.shape),
            held(seg_row.shape),
            pair_block(rows),
            held(b_vals.shape),
            held(c_vals.shape),
            pair_block(rows),
            pair_block(1),
            pair_block(ST),
        ],
        out_specs=(pair_block(rows), pair_block(rows)),
        scratch_shapes=[pltpu.VMEM((rows // span, span, span), F32)],
        compiler_params=params("arbitrary"),
        name="ssm_forward",
    )(pack, flip, seg_col, seg_row, x, b_vals, c_vals, z, skip_wide, enter)


def ssm_gate_back_kernel(
    far_ref, dg_ref, y_ref, z_ref, c_ref, flow_ref, dz_ref, dy_ref, state_ref
):
    j = pl.program_id(0)
    far = pltpu.roll(far_ref[...], lax.rem(LANES - 2 * j, LANES), 1)
    z = z_ref[...]
    sigmoid = jax.nn.sigmoid(z)
    d_gated = dg_ref[...].astype(F32)
    dy = d_gated * (z * sigmoid)
    dz_ref[...] = (d_gated * y_ref[...] * sigmoid * (1.0 + z * (1.0 - sigmoid))).astype(BF16)
    dy_ref[...] = dy.astype(BF16)
    entered = (pair_wide(far, 0) * dy).astype(BF16)
    state_ref[:ST, :] = mm(c_ref[...], entered, TN).astype(BF16)
    state_ref[ST:, :] = flow_ref[...]


def ssm_gate_back(far, d_gated, y, z, c_vals, flow, after=()):
    rows = y.shape[0]
    return pl.pallas_call(
        behind(ssm_gate_back_kernel, 6, len(after)),
        grid=(PAIRS,),
        out_shape=(
            jax.ShapeDtypeStruct((rows, D_SSM), BF16),
            jax.ShapeDtypeStruct((rows, D_SSM), BF16),
            jax.ShapeDtypeStruct((ST + FLOW_ROWS, D_SSM), BF16),
        ),
        in_specs=[
            held(far.shape),
            pair_block(rows),
            pair_block(rows),
            pair_block(rows),
            held(c_vals.shape),
            pair_block(FLOW_ROWS),
        ]
        + anywhere(len(after)),
        out_specs=(pair_block(rows), pair_block(rows), pair_block(ST + FLOW_ROWS)),
        compiler_params=params("arbitrary"),
        name="ssm_gate_back",
    )(far, d_gated, y, z, c_vals, flow, *after)


def ssm_back_kernel(
    pack_ref, flip_ref, segc_ref, segr_ref, x_ref, dy_ref, b_ref, c_ref, skip_ref, enter_ref,
    leave_ref, dtr_ref, bias_ref, alog_ref, dx_ref, db_ref, dc_ref, ddt_ref, sums_ref,
    inner_s, d_inner_s, col_s, row_s, direct_s, db_s, dc_s, skip_s,
):
    rows = x_ref.shape[0]
    span = chunk_of(rows)
    count = rows // span
    j = pl.program_id(0)
    lane = lax.broadcasted_iota(jnp.int32, (span, LANES), 1)
    first = lane < PD

    @pl.when(j == 0)
    def begin():
        for c in range(count):
            at = slice(c * span, (c + 1) * span)
            mask = same_lower(segc_ref[at, :], segr_ref[:, at], span, True)
            inner_s[c] = jnp.where(mask, mm(b_ref[at, :], c_ref[at, :], NT), 0.0)
        d_inner_s[...] = jnp.zeros(d_inner_s.shape, F32)
        col_s[...] = jnp.zeros(col_s.shape, F32)
        row_s[...] = jnp.zeros(row_s.shape, F32)
        direct_s[...] = jnp.zeros(direct_s.shape, F32)
        db_s[...] = jnp.zeros(db_s.shape, F32)
        dc_s[...] = jnp.zeros(dc_s.shape, F32)
        skip_s[...] = jnp.zeros(skip_s.shape, F32)

    packs = [
        pltpu.roll(pack_ref[c * span : (c + 1) * span, :], lax.rem(LANES - 2 * j, LANES), 1)
        for c in range(count)
    ]
    skip = skip_ref[:, :]
    states = [enter_ref[...]]
    for c in range(count - 1):
        at = slice(c * span, (c + 1) * span)
        last = pair_wide(packs[c], LANE_KEEP)[span - 1 : span, :]
        weight = pair_wide(packs[c], LANE_DT) * pair_wide(packs[c], LANE_TAIL)
        fresh = mm(b_ref[at, :], (weight * x_ref[at, :].astype(F32)).astype(BF16), TN)
        states.append(last * states[c] + fresh)
    later = leave_ref[...]
    for c in reversed(range(count)):
        at = slice(c * span, (c + 1) * span)
        pack, state = packs[c], states[c]
        b_vals, c_vals = b_ref[at, :], c_ref[at, :]
        x = x_ref[at, :].astype(F32)
        dy_low = dy_ref[at, :]
        dy = dy_low.astype(F32)
        dt = pair_wide(pack, LANE_DT)
        keep = pair_wide(pack, LANE_KEEP)
        tail = pair_wide(pack, LANE_TAIL)
        scaled = dt * x
        scaled_low = scaled.astype(BF16)
        state_low, later_low = state.astype(BF16), later.astype(BF16)
        kept_low = (keep * dy).astype(BF16)
        entered = keep * mm(c_vals, state_low)
        d_scaled_later = tail * mm(b_vals, later_low)
        dc_s[at, :] += mm(kept_low, state_low, NT)
        db_s[at, :] += mm((tail * scaled).astype(BF16), later_low, NT)
        parts, squares = [], []
        for k in range(2):
            column = pack[:, LANE_CUM + k : LANE_CUM + k + 1]
            row = flip_ref[pl.ds(LANE_CUM + 2 * j + k, 1), at]
            decay = jnp.exp(jnp.minimum(row - column, 0.0))
            mixing = inner_s[c] * decay
            own = jnp.where(first if k == 0 else ~first, scaled, 0.0).astype(BF16)
            d_mixing = mm(own, dy_low, NT)
            d_inner_s[c] += d_mixing * decay
            parts.append(mm(mixing.astype(BF16), dy_low))
            square = d_mixing * mixing
            squares.append(jnp.sum(square, axis=1, keepdims=True))
            row_s[pl.ds(2 * j + k, 1), at] = jnp.sum(square, axis=0, keepdims=True)
        d_scaled = jnp.where(first, parts[0], parts[1]) + d_scaled_later
        dx_ref[at, :] = (dt * d_scaled + skip * dy).astype(BF16)
        crossing = state * later
        crossing = jnp.sum(crossing, axis=0, keepdims=True) * keep[span - 1 : span, :]
        through = entered * dy
        leaving = scaled * d_scaled_later
        touching = x * d_scaled
        skipped = jnp.sum(dy * x, axis=0, keepdims=True)
        at_end = lax.broadcasted_iota(jnp.int32, (span, 1), 0) == span - 1
        for k in range(2):
            own = first if k == 0 else ~first
            own_row = own[:1, :]

            def side(value):
                return jnp.sum(jnp.where(own, value, 0.0), axis=1, keepdims=True)

            def side_row(value):
                return jnp.sum(jnp.where(own_row, value, 0.0), axis=1, keepdims=True)

            left = side(leaving)
            column = side(through) - left - squares[k]
            ending = jnp.sum(left, axis=0, keepdims=True) + side_row(crossing)
            column = column + jnp.where(at_end, ending, 0.0)
            mine = lane == 2 * j + k
            col_s[at, :] = jnp.where(mine, column, col_s[at, :])
            direct_s[at, :] = jnp.where(mine, side(touching), direct_s[at, :])
            skip_s[...] += jnp.where(mine[:8, :], side_row(skipped), 0.0)
        if c > 0:
            later = keep[span - 1 : span, :] * later + mm(c_vals, kept_low, TN)

    @pl.when(j == pl.num_programs(0) - 1)
    def end():
        upper = triangle(span, False)
        rate = jnp.exp(alog_ref[...])
        bias_sum = jnp.zeros((1, MH), F32)
        log_sum = jnp.zeros((1, MH), F32)
        for c in range(count):
            at = slice(c * span, (c + 1) * span)
            mask = same_lower(segc_ref[at, :], segr_ref[:, at], span, True)
            d_inner = jnp.where(mask, d_inner_s[c], 0.0).astype(BF16)
            db_ref[at, :] = (db_s[at, :] + mm(d_inner, c_ref[at, :])).astype(BF16)
            dc_ref[at, :] = (dc_s[at, :] + mm(d_inner, b_ref[at, :], TN)).astype(BF16)
            d_cum = col_s[at, :] + jnp.transpose(row_s[:, at])
            d_log = mm(upper, d_cum, precision=HIGH)[:, :MH]
            dt = pack_ref[at, :MH]
            d_dt = direct_s[at, :MH] - rate * d_log
            d_raw = d_dt * jax.nn.sigmoid(dtr_ref[at, :] + bias_ref[...])
            ddt_ref[at, :] = d_raw.astype(BF16)
            bias_sum = bias_sum + jnp.sum(d_raw, axis=0, keepdims=True)
            log_sum = log_sum - jnp.sum(d_log * dt, axis=0, keepdims=True) * rate
        sums_ref[0:1, :] = bias_sum
        sums_ref[1:2, :] = log_sum
        sums_ref[2:3, :] = skip_s[0:1, :MH]


def ssm_back(
    pack, flip, seg_col, seg_row, x, dy, b_vals, c_vals, skip_wide, enter, leave, dt_raw, bias,
    a_log, after=(),
):
    rows = x.shape[0]
    span = chunk_of(rows)
    square = pltpu.VMEM((rows // span, span, span), F32)
    tall = pltpu.VMEM((rows, LANES), F32)
    return pl.pallas_call(
        behind(ssm_back_kernel, 14, len(after)),
        grid=(PAIRS,),
        out_shape=(
            jax.ShapeDtypeStruct((rows, D_SSM), BF16),
            jax.ShapeDtypeStruct((rows, ST), BF16),
            jax.ShapeDtypeStruct((rows, ST), BF16),
            jax.ShapeDtypeStruct((rows, MH), BF16),
            jax.ShapeDtypeStruct((3, MH), F32),
        ),
        in_specs=[
            held(pack.shape),
            held(flip.shape),
            held(seg_col.shape),
            held(seg_row.shape),
            pair_block(rows),
            pair_block(rows),
            held(b_vals.shape),
            held(c_vals.shape),
            pair_block(1),
            pair_block(ST),
            pair_block(ST),
            held(dt_raw.shape),
            held(bias.shape),
            held(a_log.shape),
        ]
        + anywhere(len(after)),
        out_specs=(
            pair_block(rows),
            held((rows, ST)),
            held((rows, ST)),
            held((rows, MH)),
            held((3, MH)),
        ),
        scratch_shapes=[
            square, square, tall, pltpu.VMEM((LANES, rows), F32), tall, tall, tall,
            pltpu.VMEM((8, LANES), F32),
        ],
        compiler_params=params("arbitrary"),
        name="ssm_back",
    )(
        pack, flip, seg_col, seg_row, x, dy, b_vals, c_vals, skip_wide, enter, leave, dt_raw,
        bias, a_log, *after,
    )


def gather_rows(shard):
    groups = lax.axis_size("ctx")
    part = shard.shape[0] // groups
    own = lax.dynamic_slice_in_dim(shard, lax.axis_index("ctx") * part, part, 0)
    return lax.all_gather(own, ("fsdp", "ctx"), axis=0, tiled=True)


def from_before(value, distance):
    count = lax.axis_size("ctx")
    return lax.ppermute(value, "ctx", [(i, i + distance) for i in range(count - distance)])


def from_after(value, distance):
    count = lax.axis_size("ctx")
    return lax.ppermute(value, "ctx", [(i + distance, i) for i in range(count - distance)])


def across(value, axis, bit):
    count = lax.axis_size(axis)
    return lax.ppermute(value, axis, [(i, i ^ bit) for i in range(count)])


def pick(value, index, axis):
    return lax.dynamic_index_in_dim(value, index, axis, keepdims=False)


def sum_everywhere(value):
    for axis in ("fsdp", "ctx"):
        bit = 1
        while bit < lax.axis_size(axis):
            value = value + across(value, axis, bit)
            bit *= 2
    return value


def reduce_rows(grad):
    share = lax.psum_scatter(grad, "fsdp", scatter_dimension=0, tiled=True)
    return lax.psum(share, "ctx").astype(F32)


def spread_kernel(where_ref, *refs, shapes):
    many = len(shapes)
    owns, theirs, outs = refs[:many], refs[many : 2 * many], refs[2 * many :]
    send_top, keep_top, send_low, keep_low = outs
    y, x = where_ref[1], where_ref[2]
    base = 0
    for own, their, (part, columns) in zip(owns, theirs, shapes):
        for col in range(0, columns, LANES):
            at = slice(col, min(col + LANES, columns))
            wide = at.stop - at.start
            to = slice(base, base + part)

            def total(h, iy, ix):
                left = own[h, 0, iy, ix, :, at].astype(F32)
                return (left + their[h, 0, iy, ix, :, at].astype(F32)).astype(BF16)

            for e in range(2):
                send_top[0, e, to, :wide] = total(0, 1 - y, e)
                keep_top[0, e, to, :wide] = total(0, y, e)
                send_low[0, e, to, :wide] = total(1, e, 1 - x)
                keep_low[0, e, to, :wide] = total(1, e, x)
            base += part


def lanes_of(columns):
    return -(-columns // LANES)


def spread(where, owns, theirs):
    shapes = [a.shape[-2:] for a in owns]
    height = sum(part * lanes_of(columns) for part, columns in shapes)
    halves = owns[0].shape[0] // 2
    split = [a.reshape((2, halves) + a.shape[1:]) for a in (*owns, *theirs)]
    out = jax.ShapeDtypeStruct((halves, 2, height, LANES), BF16)
    out_block = pl.BlockSpec((1, 2, height, LANES), lambda i: (i, 0, 0, 0))
    return pl.pallas_call(
        functools.partial(spread_kernel, shapes=shapes),
        grid=(halves,),
        out_shape=(out,) * 4,
        in_specs=[smem()]
        + [
            pl.BlockSpec((2, 1) + a.shape[2:], lambda i: (0, i, 0, 0, 0, 0))
            for a in split
        ],
        out_specs=(out_block,) * 4,
        compiler_params=params("arbitrary"),
        name="spread",
    )(where, *split)


def narrow_kernel(where_ref, kt, rt, kl, rl, send_top, keep_top, send_low, keep_low):
    y, x = where_ref[1], where_ref[2]
    for keep, got, at, send_out, keep_out in (
        (kt, rt, x, send_top, keep_top),
        (kl, rl, y, send_low, keep_low),
    ):
        for target, index in ((send_out, 1 - at), (keep_out, at)):
            total = keep[0, index].astype(F32) + got[0, index].astype(F32)
            target[0] = total.astype(BF16)


def narrow(where, keep_top, got_top, keep_low, got_low):
    halves, _, height, _ = keep_top.shape
    out = jax.ShapeDtypeStruct((halves, height, LANES), BF16)
    in_block = pl.BlockSpec((1, 2, height, LANES), lambda i: (i, 0, 0, 0))
    out_block = pl.BlockSpec((1, height, LANES), lambda i: (i, 0, 0))
    return pl.pallas_call(
        narrow_kernel,
        grid=(halves,),
        out_shape=(out,) * 4,
        in_specs=[smem()] + [in_block] * 4,
        out_specs=(out_block,) * 4,
        compiler_params=params("arbitrary"),
        name="narrow",
    )(where, keep_top, got_top, keep_low, got_low)


def line_kernel(where_ref, kt, rt, kl, rl, *outs):
    z = where_ref[0]
    halves = kt.shape[0]
    count = 2 * halves
    for i in range(halves):
        for half, (keep, got) in enumerate(((kt, rt), (kl, rl))):
            total = (keep[i].astype(F32) + got[i].astype(F32)).astype(BF16)
            for d in range(count):

                @pl.when(lax.rem(z + d, count) == half * halves + i)
                def store():
                    outs[d][...] = total


def line(where, keep_top, got_top, keep_low, got_low):
    halves, height, _ = keep_top.shape
    out = jax.ShapeDtypeStruct((height, LANES), BF16)
    return pl.pallas_call(
        line_kernel,
        out_shape=(out,) * (2 * halves),
        in_specs=[smem()] + [whole()] * 4,
        out_specs=(whole(),) * (2 * halves),
        compiler_params=params(),
        name="line",
    )(where, keep_top, got_top, keep_low, got_low)


def total_kernel(*refs):
    total = refs[0][...].astype(F32)
    for ref in refs[1:-1]:
        total = total + ref[...].astype(F32)
    refs[-1][...] = total.astype(BF16)


def total_of(pieces):
    return pl.pallas_call(
        total_kernel,
        out_shape=jax.ShapeDtypeStruct(pieces[0].shape, BF16),
        in_specs=[whole()] * len(pieces),
        out_specs=whole(),
        compiler_params=params(),
        name="total",
    )(*pieces)


def place_kernel(where_ref, *refs, shapes, count):
    parts, outs = refs[:count], refs[count:]
    place = 2 * where_ref[1] + where_ref[2]
    for d, ref in enumerate(parts):
        base = 0
        for out, (part, columns) in zip(outs, shapes):
            rows = pl.ds(pl.multiple_of((place ^ d) * part, part), part)
            for col in range(0, columns, LANES):
                at = slice(col, min(col + LANES, columns))
                out[rows, at] = ref[base : base + part, : at.stop - at.start].astype(F32)
                base += part


def place_rows(where, pieces, shapes):
    count = len(pieces)
    return pl.pallas_call(
        functools.partial(place_kernel, shapes=shapes, count=count),
        out_shape=tuple(jax.ShapeDtypeStruct((count * r, c), F32) for r, c in shapes),
        in_specs=[smem()] + [whole()] * count,
        out_specs=(whole(),) * len(shapes),
        compiler_params=params(),
        name="place_rows",
    )(where, *pieces)


def along_z(value, distance):
    count = lax.axis_size("fsdp")
    hop = 2 * distance
    return lax.ppermute(value, "fsdp", [(i, (i + hop) % count) for i in range(count)])


class Reduction:
    def __init__(self, where, owns, theirs):
        self.where = where
        self.owns = owns
        self.shapes = [a.shape[-2:] for a in owns]
        self.theirs = [across(a, "fsdp", 1) for a in theirs]

    def spread(self):
        send_top, self.keep_top, send_low, self.keep_low = spread(
            self.where, self.owns, self.theirs
        )
        self.got_top, self.got_low = across(send_top, "ctx", 2), across(send_low, "ctx", 1)
        return self.keep_top

    def narrow(self):
        send_top, self.keep_top, send_low, self.keep_low = narrow(
            self.where, self.keep_top, self.got_top, self.keep_low, self.got_low
        )
        self.got_top, self.got_low = across(send_top, "ctx", 1), across(send_low, "ctx", 2)
        return self.keep_top

    def line(self):
        pieces = line(self.where, self.keep_top, self.got_top, self.keep_low, self.got_low)
        self.pieces = [pieces[0]] + [along_z(p, d) for d, p in enumerate(pieces) if d]
        return pieces[0]

    def total(self):
        share = total_of(self.pieces)
        self.shares = [share] + [across(share, "ctx", d) for d in range(1, 4)]
        return share

    def finish(self):
        return place_rows(self.where, self.shares, self.shapes)


def rms_forward(value_rows, gain):
    inverse = lax.rsqrt(jnp.mean(value_rows * value_rows, axis=-1, keepdims=True) + EPS)
    return (value_rows * inverse * gain, inverse)


def rms_backward(value_rows, inverse, gain, grad):
    weighted = grad * gain
    gain_grad = jnp.sum(grad * value_rows * inverse, axis=0)
    inner = jnp.mean(weighted * value_rows, axis=-1, keepdims=True)
    return (inverse * weighted - value_rows * inverse * inverse * inverse * inner, gain_grad)


def rope_tables(positions):
    half = HEAD_WIDTH // 2
    lane = jnp.arange(LANES)
    freqs = ROPE_BASE ** (-((lane % half).astype(F32) * 2.0) / HEAD_WIDTH)
    angles = positions.astype(F32)[:, None] * freqs[None, :]
    sign = jnp.where(lane % HEAD_WIDTH < half, -1.0, 1.0)
    return (jnp.cos(angles), jnp.sin(angles) * sign[None, :])


def chain(packed):
    state = jnp.zeros((ST, D_SSM), F32)
    for item in reversed(packed):
        own = item.astype(F32)
        flow = own[ST : ST + 1] + own[ST + 1 : ST + 2] + own[ST + 2 : ST + 3]
        state = own[:ST] + flow * state
    return state


def dotf(left, right):
    return jnp.dot(left, right, preferred_element_type=F32)


def shards(
    hidden_in, seg_ids, gain_mixer, gain_ffn, w_in, w_qkv, w_attn_out, w_ssm_out, w_gate_up,
    w_down, dt_bias, a_log, d_skip, out_grad,
):
    rows = hidden_in.shape[0]
    groups = lax.axis_size("ctx")
    place = lax.axis_index("ctx")
    full_first = gather_rows(jnp.concatenate([w_qkv, w_in], axis=1))
    full_attn_out = gather_rows(w_attn_out)
    full_ssm_out = gather_rows(w_ssm_out)
    full_gate_up = gather_rows(w_gate_up)
    full_down = gather_rows(w_down)

    seg_before = [seg_ids] + [from_before(seg_ids, k) for k in range(1, groups)]
    start = jnp.zeros((rows,), jnp.int32)
    for k in range(groups):
        earlier = (seg_before[k][None, :] < seg_ids[:, None]) & (k <= place)
        start = start + jnp.sum(earlier.astype(jnp.int32), axis=1)
    positions = place * rows + jnp.arange(rows, dtype=jnp.int32) - start
    prev_seg = jnp.where(place > 0, seg_before[1][-1:], -1).astype(jnp.int32)
    place_array = place.astype(jnp.int32).reshape(1)
    start_row = start.reshape(1, rows)
    seg_col = seg_ids.reshape(rows, 1)
    seg_row = seg_ids.reshape(1, rows)
    bias = dt_bias.reshape(1, MH)
    rates = a_log.reshape(1, MH)
    skip_wide = jnp.repeat(d_skip, PD).reshape(1, D_SSM)
    cos, sin = rope_tables(positions)

    inputs = hidden_in.astype(F32)
    normed, inverse_mixer = rms_forward(inputs, gain_mixer)
    normed_low = normed.astype(BF16)
    qkv_cols = w_qkv.shape[1]
    at_z, at_xbc = qkv_cols, qkv_cols + D_SSM
    at_dt = at_xbc + D_SSM + 2 * ST
    qkv = dotf(normed_low, full_first[:, :at_z])
    xbc = dotf(normed_low, full_first[:, at_xbc:at_dt]).astype(BF16)
    ssm_x, ssm_b, ssm_c = xbc[:, :D_SSM], xbc[:, D_SSM : D_SSM + ST], xbc[:, D_SSM + ST :]
    dt_raw = dotf(normed_low, full_first[:, at_dt:])
    gate_z = dotf(normed_low, full_first[:, at_z:at_xbc])
    q, kv = rotate(qkv, cos, sin)
    kv_all = jnp.stack([kv] + [from_before(kv, k) for k in range(1, groups)])
    pack, flip, far, end_state = ssm_state(prev_seg, dt_raw, bias, rates, seg_col, ssm_x, ssm_b)
    enter = chain([from_before(end_state, k) for k in range(1, groups)])

    attended, lse = attend(place_array, q, kv_all, start_row)
    attended_low = attended.astype(BF16)
    gated_low, y = ssm_forward(
        pack, flip, seg_col, seg_row, ssm_x, ssm_b, ssm_c, gate_z, skip_wide, enter
    )
    middle = inputs + dotf(attended_low, full_attn_out) + dotf(gated_low, full_ssm_out)
    normed_ffn, inverse_ffn = rms_forward(middle, gain_ffn)
    normed_ffn_low = normed_ffn.astype(BF16)
    gate = dotf(normed_ffn_low, full_gate_up[:, :FF])
    up = dotf(normed_ffn_low, full_gate_up[:, FF:])
    sigmoid_gate = jax.nn.sigmoid(gate)
    hidden_low = (gate * sigmoid_gate * up).astype(BF16)
    output = (middle + dotf(hidden_low, full_down)).astype(BF16)

    staged = groups == 4 and lax.axis_size("fsdp") == 8
    fsdp_place = lax.axis_index("fsdp")
    core = fsdp_place % 2
    where = jnp.stack([fsdp_place // 2, place // 2, place % 2]).astype(jnp.int32)

    def sides(left):
        width = left.shape[1] // lax.axis_size("fsdp")
        split = left.reshape(rows, -1, 2, width)
        return tuple(pick(split, k, 2).reshape(rows, -1) for k in (core, 1 - core))

    def split(grad):
        lines, part = lax.axis_size("fsdp") // 2, grad.shape[0] // 16
        return grad.reshape(lines, 2, 2, part, grad.shape[1])

    def product(own_other, right):
        own, other = own_other
        theirs = split(dotf(other.T, right).astype(BF16))
        return (split(dotf(own.T, right).astype(BF16)), theirs)

    def parted(left, right):
        grad = dotf(left.T, right).astype(BF16)
        both = grad.reshape(-1, 2, 2, 2, grad.shape[0] // 32, grad.shape[1])
        return (pick(both, core, 1), pick(both, 1 - core, 1))

    def begin(pairs):
        owns, theirs = zip(*pairs, strict=True)
        return Reduction(where, owns, theirs)

    hold = lambda step: (step(),) if staged else ()
    normed_sides = sides(normed_low)
    d_hidden = dotf(out_grad, full_down.T)
    d_gate = (d_hidden * up * sigmoid_gate * (1.0 + gate * (1.0 - sigmoid_gate))).astype(BF16)
    d_up = (d_hidden * gate * sigmoid_gate).astype(BF16)
    d_gate_up = jnp.concatenate([d_gate, d_up], axis=1)
    if staged:
        one = begin(
            [product(sides(hidden_low), out_grad), product(sides(normed_ffn_low), d_gate_up)]
        )
    d_normed_ffn = dotf(d_gate_up, full_gate_up.T)
    middle_part, grad_gain_ffn = rms_backward(middle, inverse_ffn, gain_ffn, d_normed_ffn)
    d_middle = out_grad.astype(F32) + middle_part
    d_branch = d_middle.astype(BF16)
    d_attended = dotf(d_branch, full_attn_out.T).astype(BF16)
    d_gated = dotf(d_branch, full_ssm_out.T).astype(BF16)

    dz, dy, state_grad = ssm_gate_back(far, d_gated, y, gate_z, ssm_c, end_state[ST:])
    leave = chain([from_after(state_grad, k) for k in range(1, groups)])
    if staged:
        two = begin(
            [
                parted(attended_low, d_branch),
                parted(gated_low, d_branch),
                product(normed_sides, dz),
            ]
        )
    dq, dkv_all = attend_back(
        place_array, q, kv_all, start_row, lse, attended, d_attended,
        after=hold(lambda: one.spread()),
    )
    dkv = dkv_all[0].astype(F32)
    for k in range(1, groups):
        dkv = dkv + from_after(dkv_all[k], k).astype(F32)
    dx, db, dc, ddt, sums = ssm_back(
        pack, flip, seg_col, seg_row, ssm_x, dy, ssm_b, ssm_c, skip_wide, enter, leave, dt_raw,
        bias, rates, after=hold(lambda: one.narrow()) + hold(lambda: two.spread()),
    )
    d_qkv = unrotate(dq, dkv, cos, sin)
    d_late = jnp.concatenate([dx, db, dc, ddt], axis=1)
    if staged:
        three = begin([product(normed_sides, d_qkv), product(normed_sides, d_late)])
        one.line()
        two.narrow()
        three.spread()
    d_early = jnp.concatenate([d_qkv, dz], axis=1)
    d_normed = dotf(d_early, full_first[:, :at_xbc].T) + dotf(d_late, full_first[:, at_xbc:].T)
    input_part, grad_gain_mixer = rms_backward(inputs, inverse_mixer, gain_mixer, d_normed)
    grad_input = d_middle + input_part
    small = jnp.concatenate([sums.reshape(-1), grad_gain_mixer, grad_gain_ffn])
    small = sum_everywhere(small)
    head_sums = small[: 3 * MH].reshape(3, MH)
    gains = small[3 * MH :].reshape(2, lax.axis_size("fsdp"), -1)
    gains = pick(gains, fsdp_place, 1)
    if staged:
        one.total()
        two.line()
        three.narrow()
        two.total()
        three.line()
        three.total()
        out_down, out_gate_up = one.finish()
        out_attn, out_ssm, out_z = two.finish()
        out_qkv, out_late = three.finish()
    else:
        out_down = reduce_rows(dotf(hidden_low.T, out_grad).astype(BF16))
        out_gate_up = reduce_rows(dotf(normed_ffn_low.T, d_gate_up).astype(BF16))
        out_attn = reduce_rows(dotf(attended_low.T, d_branch).astype(BF16))
        out_ssm = reduce_rows(dotf(gated_low.T, d_branch).astype(BF16))
        out_z = reduce_rows(dotf(normed_low.T, dz).astype(BF16))
        out_qkv = reduce_rows(dotf(normed_low.T, d_qkv).astype(BF16))
        out_late = reduce_rows(dotf(normed_low.T, d_late).astype(BF16))
    return (
        output,
        grad_input,
        gains[0],
        gains[1],
        jnp.concatenate([out_z, out_late], axis=1),
        out_qkv,
        out_attn,
        out_ssm,
        out_gate_up,
        out_down,
        head_sums[0],
        head_sums[1],
        head_sums[2],
    )


def solution(mesh):
    tokens = P(("fsdp", "ctx"), None)
    weight = P("fsdp", None)
    return jax.shard_map(
        shards,
        mesh=mesh,
        in_specs=(
            tokens, P(("fsdp", "ctx")), P(), P(), weight, weight, weight, weight, weight, weight,
            P(), P(), P(), tokens,
        ),
        out_specs=(
            tokens, tokens, P("fsdp"), P("fsdp"), weight, weight, weight, weight, weight, weight,
            P(), P(), P(),
        ),
        check_vma=False,
    )
```
